32 devices in a mesh: seq: 8 (over z, x), head: 4 (over y, core).
Axes of the slice: x: 2, y: 2, z: 4, core: 2. Of those that a mesh axis runs over, the one named last changes fastest.
Arguments:
- tokens: bfloat16 [16384, 2048], P('seq'), may hold values from -6 to 6
- norm_gain: float32 [2048], replicated, may hold values from 0.5 to 2
- in_weight: bfloat16 [2048, 3, 2048], P(None, None, 'head')
- out_weight: bfloat16 [2048, 2048], P('head'), may hold values from -0.125 to 0.125
- pattern: int32 [128, 4], replicated, may hold values from 0 to 127, as said below
Outputs:
- mixed: bfloat16 [16384, 2048], P(('seq', 'head'))
The draws below stay inside these ranges and needn't reach their ends.
Inputs may be any that keep to these rules, and one draw needn't show every extreme that they name: `pattern`: row i names first tile i itself, then 4 - 1 distinct tiles held by other indices of seq (index = tile // 16). Among the rows of one index of seq, at most 10 of these later entries name tiles of any one other index, and every index has one such other index that it names exactly 10 times.
All inputs are finite; a program needn't handle non-finite values.
Results may differ from the reference program's by a relative error of at most 0.019.
Values may be sent and summed in bfloat16 or wider, within the bound.
A program may use at most 128 MiB of HBM per device.

```python
import math
import jax
import jax.numpy as jnp
from jax import lax

D = 2048
H = 16
HD = 128
TILE = 128
KT = 4
SHARDS = 8
TOKENS = 16384
QT_DEV = 16
CAP = 10


def draw_in_weight(key, part):
    key_query, key_key, key_value = jax.random.split(key, 3)
    query_weight = jax.random.normal(key_query, (D, H * HD), jnp.float32) / jnp.sqrt(jnp.float32(D))
    value_weight = jax.random.normal(key_value, (D, H * HD), jnp.float32) / jnp.sqrt(jnp.float32(D))
    noise_weight = jax.random.normal(key_key, (D, H * HD), jnp.float32) / jnp.sqrt(jnp.float32(D))
    key_weight = noise_weight
    return jnp.stack([query_weight, key_weight, value_weight], axis=1).astype(jnp.bfloat16)


def draw_pattern(key, part):
    entries = QT_DEV * (KT - 1)
    slot_total = (SHARDS - 1) * CAP

    def for_device(device):
        device_key = jax.random.fold_in(key, device)
        key_hub, key_order, key_base = jax.random.split(device_key, 3)
        hub_offset = jax.random.randint(key_hub, (), 1, SHARDS)
        counter = jnp.arange(slot_total, dtype=jnp.int32)
        offsets = 1 + counter // CAP
        shuffled = jax.random.permutation(key_order, slot_total).astype(jnp.int32)
        ranking = jnp.where(offsets == hub_offset, -1 - counter % CAP, shuffled)
        order = jnp.argsort(ranking, stable=True)
        picked = offsets[order][:entries]
        owners = (device + picked) % SHARDS
        bases = jax.random.randint(key_base, (SHARDS,), 0, QT_DEV)
        position = jnp.arange(entries, dtype=jnp.int32)
        row_pos = position // (KT - 1)
        slot_pos = position % (KT - 1) + 1
        local_tile = (bases[owners] + row_pos + slot_pos) % QT_DEV
        remote = (owners * QT_DEV + local_tile).reshape(QT_DEV, KT - 1)
        own_tiles = device * QT_DEV + jnp.arange(QT_DEV, dtype=jnp.int32)
        return jnp.concatenate([own_tiles[:, None], remote], axis=1)
    table = jax.vmap(for_device)(jnp.arange(SHARDS, dtype=jnp.int32))
    return table.reshape(SHARDS * QT_DEV, KT).astype(jnp.int32)


def shard_levels(rng, shape, cuts, smallest, largest):
    factor_of = 1.0
    for axis_at, parts in cuts:
        steps = jax.random.uniform(jax.random.fold_in(jax.random.fold_in(rng, 6), axis_at), (parts,), jnp.float32, smallest / len(cuts), largest / len(cuts))
        factor_of = factor_of * jnp.repeat(jnp.exp(steps), shape[axis_at] // parts).reshape((-1,) + (1,) * (len(shape) - 1 - axis_at))
    return factor_of


def centred(key, shape, width, reach, pieces=(), held_as=jnp.bfloat16):
    drawn = width * jax.random.normal(key, shape, jnp.float32)
    if pieces:
        drawn = drawn * shard_levels(key, shape, pieces, -0.22, 0.18)
    return jnp.clip(drawn, -reach, reach).astype(held_as)


def setup_inputs(seed: int = 0) -> dict:
    arg_keys = jax.random.split(jax.random.key(seed), 6)
    return {
        "tokens": centred(arg_keys[0], (TOKENS, D), 1.0, 6.0, ((0, 8),)),
        "norm_gain": jnp.clip(jnp.exp(jax.random.uniform(arg_keys[1], (D,), jnp.float32, math.log(0.5), math.log(2.0))), 0.5, 2.0),
        "in_weight": draw_in_weight(jax.random.fold_in(arg_keys[5], 71), 0),
        "out_weight": centred(arg_keys[3], (H * HD, D), (H * HD) ** -0.5, 0.125, ((0, 4),)),
        "pattern": draw_pattern(jax.random.fold_in(arg_keys[5], 71), 0),
    }


def reference(tokens, norm_gain, in_weight, out_weight, pattern):
    values = tokens.astype(jnp.float32)
    mean_square = lax.optimization_barrier(jnp.mean(values * values, axis=-1, keepdims=True))
    normed = (values * lax.rsqrt(mean_square + 1e-05) * norm_gain).astype(jnp.bfloat16)
    projected = jnp.dot(normed, in_weight.reshape(D, 3 * H * HD), preferred_element_type=jnp.float32).astype(jnp.bfloat16)
    projected = lax.optimization_barrier(projected).reshape(TOKENS, 3, H, HD)
    tile_total = TOKENS // TILE
    query_tiles = projected[:, 0].reshape(tile_total, TILE, H, HD)
    key_tiles = projected[:, 1].reshape(tile_total, TILE, H, HD)
    value_tiles = projected[:, 2].reshape(tile_total, TILE, H, HD)
    scale = 1.0 / math.sqrt(HD)

    def one_tile(index):
        chosen = pattern[index]
        query_block = query_tiles[index].astype(jnp.float32)
        key_block = key_tiles[chosen].reshape(KT * TILE, H, HD).astype(jnp.float32)
        value_block = value_tiles[chosen].reshape(KT * TILE, H, HD).astype(jnp.float32)
        scores = jnp.einsum('qhd,khd->hqk', query_block, key_block) * scale
        maxima = lax.optimization_barrier(jnp.max(scores, axis=-1, keepdims=True))
        exponent = jnp.exp(scores - maxima)
        weights = (exponent / lax.optimization_barrier(jnp.sum(exponent, axis=-1, keepdims=True))).astype(jnp.bfloat16)
        weights = lax.optimization_barrier(weights).astype(jnp.float32)
        return jnp.einsum('hqk,khd->qhd', weights, value_block).astype(jnp.bfloat16)
    attended = lax.map(one_tile, jnp.arange(tile_total, dtype=jnp.int32)).reshape(TOKENS, H * HD)
    return jnp.dot(attended, out_weight, preferred_element_type=jnp.float32).astype(jnp.bfloat16)
```

```python
import math

import jax
import jax.numpy as jnp
from jax import lax
from jax.experimental import pallas as pl
from jax.experimental.pallas import tpu as pltpu
from jax.sharding import Mesh
from jax.sharding import PartitionSpec as P

HD = 128
TILE = 128
KT = 4
ZS, XS, YS, CS = 4, 2, 2, 2
PARTS = YS * CS
ORDER = ((0, 1, 2, 3), (1, 0, 2, 3), (2, 3, 1, 0), (3, 2, 1, 0))
SWAP = ((0, 1), (1, 0))
OWN_SLOTS = 20
VMEM = 48 * 1024 * 1024


def normalize(tokens, norm_gain):
    values = tokens.astype(jnp.float32)
    mean_square = jnp.mean(values * values, axis=-1, keepdims=True)
    return (values * lax.rsqrt(mean_square + 1e-05) * norm_gain).astype(jnp.bfloat16)


def by_request(keyvals, pattern, my_rows, shards, myself, tile_count):
    entries = tile_count * (KT - 1)
    capacity = max(2, 3 * entries // (2 * (shards - 1)))
    wanted = pattern.reshape(shards, tile_count, KT)[:, :, 1:].reshape(shards, entries)
    owners = wanted // tile_count
    local_tile = wanted % tile_count
    owned_here = owners == myself
    ranking = jnp.cumsum(owned_here.astype(jnp.int32), axis=1) - 1
    slot_ids = jnp.arange(capacity, dtype=jnp.int32)
    select = owned_here[:, None, :] & (ranking[:, None, :] == slot_ids[None, :, None])
    filled = jnp.any(select, axis=2)
    chosen = jnp.sum(jnp.where(select, local_tile[:, None, :], 0), axis=2)
    outgoing = jnp.where(filled[:, :, None, None], keyvals[chosen], jnp.zeros((), keyvals.dtype))
    incoming = lax.all_to_all(outgoing, "seq", split_axis=0, concat_axis=0, tiled=True)
    sources = my_rows[:, 1:].reshape(entries) // tile_count
    one_hot = (sources[:, None] == jnp.arange(shards, dtype=jnp.int32)[None, :]).astype(jnp.int32)
    running = jnp.cumsum(one_hot, axis=0)
    position = jnp.sum(running * one_hot, axis=1) - 1
    flat_index = sources * capacity + position
    fetched = incoming.reshape(shards * capacity, TILE, keyvals.shape[2])[flat_index]
    return fetched.reshape(tile_count, KT - 1, TILE, keyvals.shape[2])


def body(tokens, norm_gain, in_weight, out_weight, pattern):
    shards = lax.axis_size("seq")
    myself = lax.axis_index("seq")
    row_count = tokens.shape[0]
    tile_count = row_count // TILE
    head_width = in_weight.shape[2]
    head_count = head_width // HD
    normed = normalize(tokens, norm_gain)
    projected = jnp.dot(
        normed,
        in_weight.reshape(in_weight.shape[0], 3 * head_width),
        preferred_element_type=jnp.float32,
    ).astype(jnp.bfloat16)
    projected = projected.reshape(row_count, 3, head_width)
    queries = projected[:, 0].reshape(tile_count, TILE, head_count, HD)
    keyvals = jnp.concatenate([projected[:, 1], projected[:, 2]], axis=1).reshape(
        tile_count, TILE, 2 * head_width
    )
    my_rows = lax.dynamic_slice_in_dim(pattern, myself * tile_count, tile_count, 0)
    fetched = by_request(keyvals, pattern, my_rows, shards, myself, tile_count)
    gathered = jnp.concatenate([keyvals[:, None], fetched], axis=1).reshape(
        tile_count, KT * TILE, 2 * head_width
    )
    key_block = gathered[:, :, :head_width].reshape(tile_count, KT * TILE, head_count, HD)
    value_block = gathered[:, :, head_width:].reshape(tile_count, KT * TILE, head_count, HD)
    scores = jnp.einsum(
        "tqhd,tkhd->thqk", queries, key_block, preferred_element_type=jnp.float32
    ) * (1.0 / math.sqrt(HD))
    maxima = jnp.max(scores, axis=-1, keepdims=True)
    exponent = jnp.exp(scores - maxima)
    weights = (exponent / jnp.sum(exponent, axis=-1, keepdims=True)).astype(jnp.bfloat16)
    attended = jnp.einsum(
        "thqk,tkhd->tqhd", weights, value_block, preferred_element_type=jnp.float32
    ).astype(jnp.bfloat16)
    attended = attended.reshape(row_count, head_width)
    return lax.psum_scatter(
        jnp.dot(attended, out_weight, preferred_element_type=jnp.float32).astype(jnp.bfloat16),
        "head",
        scatter_dimension=0,
        tiled=True,
    )


def project_kernel(count, *refs):
    blocks, weight, out = refs[:count], refs[count], refs[-1]
    rows = jnp.concatenate([ref[...] for ref in blocks], axis=1)
    tiles, height, depth = rows.shape
    product = jnp.dot(
        rows.reshape(tiles * height, depth), weight[...], preferred_element_type=jnp.float32
    )
    out[...] = product.astype(out.dtype).reshape(tiles, height, out.shape[2])


def project(pieces, weight, slots, base, step, buffer):
    tiles, depth = pieces[0].shape[0], pieces[0].shape[2]
    width = weight.shape[1]
    in_specs = [pl.BlockSpec((step, p.shape[1], depth), lambda i: (i, 0, 0)) for p in pieces]
    in_specs.append(pl.BlockSpec((depth, width), lambda i: (0, 0)))
    operands = list(pieces) + [weight]
    aliases = {}
    if buffer is not None:
        aliases = {len(operands): 0}
        in_specs.append(pl.BlockSpec(memory_space=pl.ANY))
        operands.append(buffer)
    rows = tiles * TILE
    return pl.pallas_call(
        lambda *refs: project_kernel(len(pieces), *refs),
        grid=(tiles // step,),
        in_specs=in_specs,
        out_specs=pl.BlockSpec((step, TILE, width), lambda i: (base // step + i, 0, 0)),
        out_shape=jax.ShapeDtypeStruct((slots, TILE, width), jnp.bfloat16),
        input_output_aliases=aliases,
        compiler_params=pltpu.CompilerParams(vmem_limit_bytes=VMEM),
        cost_estimate=pl.CostEstimate(
            flops=2 * rows * depth * width,
            bytes_accessed=2 * (rows * depth + depth * width + rows * width),
            transcendentals=0,
        ),
    )(*operands)


def attend_kernel(tile_ids, slot_ids, query, *refs):
    blocks, out = refs[:KT], refs[KT]
    width = query.shape[1]
    for head in range(width // HD):
        at = slice(head * HD, (head + 1) * HD)
        at_value = slice(width + head * HD, width + (head + 1) * HD)
        keys = jnp.concatenate([ref[0, :, at] for ref in blocks], axis=0)
        values = jnp.concatenate([ref[0, :, at_value] for ref in blocks], axis=0)
        scores = lax.dot_general(
            query[:, at], keys, (((1,), (1,)), ((), ())), preferred_element_type=jnp.float32
        ) * (1.0 / math.sqrt(HD))
        exponent = jnp.exp(scores - jnp.max(scores, axis=-1, keepdims=True))
        total = jnp.sum(exponent, axis=-1, keepdims=True)
        summed = jnp.dot(
            exponent.astype(jnp.bfloat16), values, preferred_element_type=jnp.float32
        )
        out[:, at] = (summed / total).astype(out.dtype)


def attend(tile_ids, slot_ids, queries, buffer):
    tiles, width = tile_ids.shape[0], queries.shape[1]

    def at_slot(k):
        return lambda i, tile_ids, slot_ids: (slot_ids[i * KT + k], 0, 0)

    return pl.pallas_call(
        attend_kernel,
        grid_spec=pltpu.PrefetchScalarGridSpec(
            num_scalar_prefetch=2,
            grid=(tiles,),
            in_specs=[pl.BlockSpec((TILE, width), lambda i, tile_ids, slot_ids: (tile_ids[i], 0))]
            + [pl.BlockSpec((1, TILE, 2 * width), at_slot(k)) for k in range(KT)],
            out_specs=pl.BlockSpec((TILE, width), lambda i, tile_ids, slot_ids: (i, 0)),
        ),
        out_shape=jax.ShapeDtypeStruct((tiles * TILE, width), jnp.bfloat16),
        compiler_params=pltpu.CompilerParams(vmem_limit_bytes=VMEM),
        cost_estimate=pl.CostEstimate(
            flops=4 * tiles * TILE * KT * TILE * width,
            bytes_accessed=2 * tiles * TILE * width * (2 + 2 * KT),
            transcendentals=tiles * TILE * KT * TILE * (width // HD),
        ),
    )(tile_ids, slot_ids, queries, *([buffer] * KT))


def request_lists(rows, shards, tile_count, capacity):
    entries = rows.reshape(-1)
    owned = (entries // tile_count)[None, :] == jnp.arange(shards, dtype=jnp.int32)[:, None]
    rank = jnp.cumsum(owned.astype(jnp.int32), axis=1) - 1
    slot_ids = jnp.arange(capacity, dtype=jnp.int32)
    select = owned[:, None, :] & (rank[:, None, :] == slot_ids[None, :, None])
    chosen = jnp.sum(jnp.where(select, (entries % tile_count)[None, None, :], 0), axis=2)
    return chosen, jnp.sum(jnp.where(owned, rank, 0), axis=0)


def grid_body(tokens, norm_gain, in_weight, out_weight, pattern):
    shards = ZS * XS
    z, x = lax.axis_index("z"), lax.axis_index("x")
    y, c = lax.axis_index("y"), lax.axis_index("c")
    me, beside = z * XS + x, z * XS + (1 - x)
    rows, depth = tokens.shape
    tile_count = rows // TILE
    entries = tile_count * (KT - 1)
    capacity = max(2, 3 * entries // (2 * (shards - 1)))
    head_width = in_weight.shape[2]
    share = TILE // PARTS
    order = jnp.asarray(ORDER, jnp.int32)[z]

    tiles = tokens.reshape(tile_count, PARTS, share, depth)
    mine = lax.dynamic_index_in_dim(tiles, y * CS + c, 1, keepdims=False)
    block = normalize(mine, norm_gain)

    ups, downs = [block], [block]
    for s in range(1, ZS):
        ups.append(lax.ppermute(ups[-1], "z", [(i, i + 1) for i in range(s - 1, ZS - 1)]))
        downs.append(lax.ppermute(downs[-1], "z", [(i, i - 1) for i in range(1, ZS - s + 1)]))

    my_rows = lax.dynamic_slice_in_dim(pattern, me * tile_count, tile_count, 0)[:, 1:]
    beside_rows = lax.dynamic_slice_in_dim(pattern, beside * tile_count, tile_count, 0)[:, 1:]
    my_lists, my_rank = request_lists(my_rows, shards, tile_count, capacity)
    beside_lists, _ = request_lists(beside_rows, shards, tile_count, capacity)

    def column_block(k):
        parts = []
        for at in range(ZS):
            source = ORDER[at][k]
            parts.append(ups[at - source] if source <= at else downs[source - at])
        out = parts[0]
        for at in range(1, ZS):
            if parts[at] is not parts[at - 1]:
                out = jnp.where(z >= at, parts[at], out)
        return out

    pieces = []
    for k in range(ZS):
        held = block if k == 0 else column_block(k)
        source = order[k] * XS + x
        out = held[beside_lists[source]]
        came = lax.ppermute(out, "x", SWAP)
        if k:
            pieces.append(held[my_lists[source]])
        pieces.append(came)

    normed = normalize(tokens, norm_gain)
    queries = jnp.dot(
        normed, in_weight[:, 0, :], preferred_element_type=jnp.float32
    ).astype(jnp.bfloat16)
    weight = in_weight[:, 1:, :].reshape(depth, 2 * head_width)
    slots = OWN_SLOTS + capacity * len(pieces)
    buffer = project([normed.reshape(tile_count, TILE, depth)], weight, slots, 0, 4, None)
    for at, piece in enumerate(pieces):
        across = lax.ppermute(piece, "y", SWAP)
        sides = lax.ppermute(piece, "c", SWAP)
        corner = lax.ppermute(across, "c", SWAP)
        buffer = project(
            [piece, across, sides, corner], weight, slots,
            OWN_SLOTS + at * capacity, capacity // 2, buffer,
        )

    w_across = lax.ppermute(out_weight, "y", SWAP)
    w_sides = lax.ppermute(out_weight, "c", SWAP)
    w_corner = lax.ppermute(w_across, "c", SWAP)
    out_all = jnp.concatenate([out_weight, w_across, w_sides, w_corner], axis=0)

    owner = my_rows // tile_count
    step_of = jnp.sum(
        jnp.where(
            order[None, None, :] == (owner // XS)[:, :, None],
            jnp.arange(ZS, dtype=jnp.int32)[None, None, :],
            0,
        ),
        axis=2,
    )
    place = 2 * step_of - jnp.where(owner % XS == x, 1, 0)
    far_slots = OWN_SLOTS + place * capacity + my_rank.reshape(tile_count, KT - 1)
    slot_ids = jnp.concatenate(
        [jnp.arange(tile_count, dtype=jnp.int32)[:, None], far_slots], axis=1
    )

    half = tile_count // YS
    near = jnp.arange(half, dtype=jnp.int32)

    def attend_half(which):
        ids = which * half + near
        picked = lax.dynamic_slice_in_dim(slot_ids, which * half, half, 0)
        return attend(ids, picked.reshape(-1), queries, buffer)

    far = attend_half(1 - y)
    far_came = lax.ppermute(far, "y", SWAP)
    own = attend_half(y)
    quarter = own.shape[0] // CS
    keep = [lax.dynamic_slice_in_dim(a, c * quarter, quarter, 0) for a in (own, far_came)]
    give = [lax.dynamic_slice_in_dim(a, (1 - c) * quarter, quarter, 0) for a in (own, far_came)]
    came = [lax.ppermute(a, "c", SWAP) for a in give]
    attended = jnp.concatenate(keep + came, axis=1)
    return jnp.dot(attended, out_all, preferred_element_type=jnp.float32).astype(jnp.bfloat16)


def solution(mesh):
    if mesh.devices.shape == (ZS * XS, YS * CS):
        grid = Mesh(mesh.devices.reshape(ZS, XS, YS, CS), ("z", "x", "y", "c"))
        seq, head = ("z", "x"), ("y", "c")
        return jax.shard_map(
            grid_body,
            mesh=grid,
            in_specs=(P(seq, None), P(), P(None, None, head), P(head, None), P()),
            out_specs=P(seq + head, None),
            check_vma=False,
        )
    return jax.shard_map(
        body,
        mesh=mesh,
        in_specs=(P("seq", None), P(), P(None, None, "head"), P("head", None), P()),
        out_specs=P(("seq", "head"), None),
        check_vma=False,
    )
```

```python
import math

import jax
import jax.numpy as jnp
from jax import lax
from jax.experimental import pallas as pl
from jax.experimental.pallas import tpu as pltpu
from jax.sharding import Mesh
from jax.sharding import PartitionSpec as P

HD = 128
TILE = 128
KT = 4
ZS, XS, YS, CS = 4, 2, 2, 2
PARTS = YS * CS
ORDER = ((0, 1, 2, 3), (1, 0, 2, 3), (2, 3, 1, 0), (3, 2, 1, 0))
SWAP = ((0, 1), (1, 0))
OWN_SLOTS = 20
VMEM = 48 * 1024 * 1024


def normalize(tokens, norm_gain):
    values = tokens.astype(jnp.float32)
    mean_square = jnp.mean(values * values, axis=-1, keepdims=True)
    return (values * lax.rsqrt(mean_square + 1e-05) * norm_gain).astype(jnp.bfloat16)


def by_request(keyvals, pattern, my_rows, shards, myself, tile_count):
    entries = tile_count * (KT - 1)
    capacity = max(2, 3 * entries // (2 * (shards - 1)))
    wanted = pattern.reshape(shards, tile_count, KT)[:, :, 1:].reshape(shards, entries)
    owners = wanted // tile_count
    local_tile = wanted % tile_count
    owned_here = owners == myself
    ranking = jnp.cumsum(owned_here.astype(jnp.int32), axis=1) - 1
    slot_ids = jnp.arange(capacity, dtype=jnp.int32)
    select = owned_here[:, None, :] & (ranking[:, None, :] == slot_ids[None, :, None])
    filled = jnp.any(select, axis=2)
    chosen = jnp.sum(jnp.where(select, local_tile[:, None, :], 0), axis=2)
    outgoing = jnp.where(filled[:, :, None, None], keyvals[chosen], jnp.zeros((), keyvals.dtype))
    incoming = lax.all_to_all(outgoing, "seq", split_axis=0, concat_axis=0, tiled=True)
    sources = my_rows[:, 1:].reshape(entries) // tile_count
    one_hot = (sources[:, None] == jnp.arange(shards, dtype=jnp.int32)[None, :]).astype(jnp.int32)
    running = jnp.cumsum(one_hot, axis=0)
    position = jnp.sum(running * one_hot, axis=1) - 1
    flat_index = sources * capacity + position
    fetched = incoming.reshape(shards * capacity, TILE, keyvals.shape[2])[flat_index]
    return fetched.reshape(tile_count, KT - 1, TILE, keyvals.shape[2])


def body(tokens, norm_gain, in_weight, out_weight, pattern):
    shards = lax.axis_size("seq")
    myself = lax.axis_index("seq")
    row_count = tokens.shape[0]
    tile_count = row_count // TILE
    head_width = in_weight.shape[2]
    head_count = head_width // HD
    normed = normalize(tokens, norm_gain)
    projected = jnp.dot(
        normed,
        in_weight.reshape(in_weight.shape[0], 3 * head_width),
        preferred_element_type=jnp.float32,
    ).astype(jnp.bfloat16)
    projected = projected.reshape(row_count, 3, head_width)
    queries = projected[:, 0].reshape(tile_count, TILE, head_count, HD)
    keyvals = jnp.concatenate([projected[:, 1], projected[:, 2]], axis=1).reshape(
        tile_count, TILE, 2 * head_width
    )
    my_rows = lax.dynamic_slice_in_dim(pattern, myself * tile_count, tile_count, 0)
    fetched = by_request(keyvals, pattern, my_rows, shards, myself, tile_count)
    gathered = jnp.concatenate([keyvals[:, None], fetched], axis=1).reshape(
        tile_count, KT * TILE, 2 * head_width
    )
    key_block = gathered[:, :, :head_width].reshape(tile_count, KT * TILE, head_count, HD)
    value_block = gathered[:, :, head_width:].reshape(tile_count, KT * TILE, head_count, HD)
    scores = jnp.einsum(
        "tqhd,tkhd->thqk", queries, key_block, preferred_element_type=jnp.float32
    ) * (1.0 / math.sqrt(HD))
    maxima = jnp.max(scores, axis=-1, keepdims=True)
    exponent = jnp.exp(scores - maxima)
    weights = (exponent / jnp.sum(exponent, axis=-1, keepdims=True)).astype(jnp.bfloat16)
    attended = jnp.einsum(
        "thqk,tkhd->tqhd", weights, value_block, preferred_element_type=jnp.float32
    ).astype(jnp.bfloat16)
    attended = attended.reshape(row_count, head_width)
    return lax.psum_scatter(
        jnp.dot(attended, out_weight, preferred_element_type=jnp.float32).astype(jnp.bfloat16),
        "head",
        scatter_dimension=0,
        tiled=True,
    )


def project_kernel(count, *refs):
    blocks, weight, out = refs[:count], refs[count], refs[-1]
    rows = jnp.concatenate([ref[...] for ref in blocks], axis=1)
    tiles, height, depth = rows.shape
    product = jnp.dot(
        rows.reshape(tiles * height, depth), weight[...], preferred_element_type=jnp.float32
    )
    out[...] = product.astype(out.dtype).reshape(tiles, height, out.shape[2])


def project(pieces, tiles, weight, slots, base, step, buffer):
    depth, width = weight.shape

    def rows_from(array, start):
        return pl.BlockSpec((step, array.shape[1], depth), lambda i: (start // step + i, 0, 0))

    in_specs = [rows_from(*piece) for piece in pieces]
    in_specs.append(pl.BlockSpec((depth, width), lambda i: (0, 0)))
    operands = [array for array, _ in pieces] + [weight]
    aliases = {}
    if buffer is not None:
        aliases = {len(operands): 0}
        in_specs.append(pl.BlockSpec(memory_space=pl.ANY))
        operands.append(buffer)
    rows = tiles * TILE
    return pl.pallas_call(
        lambda *refs: project_kernel(len(pieces), *refs),
        grid=(tiles // step,),
        in_specs=in_specs,
        out_specs=pl.BlockSpec((step, TILE, width), lambda i: (base // step + i, 0, 0)),
        out_shape=jax.ShapeDtypeStruct((slots, TILE, width), jnp.bfloat16),
        input_output_aliases=aliases,
        compiler_params=pltpu.CompilerParams(vmem_limit_bytes=VMEM),
        cost_estimate=pl.CostEstimate(
            flops=2 * rows * depth * width,
            bytes_accessed=2 * (rows * depth + depth * width + rows * width),
            transcendentals=0,
        ),
    )(*operands)


def attend_kernel(tile_ids, slot_ids, query, *refs):
    blocks, out = refs[:KT], refs[KT]
    width = query.shape[1]
    for head in range(width // HD):
        at = slice(head * HD, (head + 1) * HD)
        at_value = slice(width + head * HD, width + (head + 1) * HD)
        keys = jnp.concatenate([ref[0, :, at] for ref in blocks], axis=0)
        values = jnp.concatenate([ref[0, :, at_value] for ref in blocks], axis=0)
        scores = lax.dot_general(
            query[:, at], keys, (((1,), (1,)), ((), ())), preferred_element_type=jnp.float32
        ) * (1.0 / math.sqrt(HD))
        exponent = jnp.exp(scores - jnp.max(scores, axis=-1, keepdims=True))
        total = jnp.sum(exponent, axis=-1, keepdims=True)
        summed = jnp.dot(
            exponent.astype(jnp.bfloat16), values, preferred_element_type=jnp.float32
        )
        out[:, at] = (summed / total).astype(out.dtype)


def attend(tile_ids, slot_ids, queries, buffer):
    tiles, width = tile_ids.shape[0], queries.shape[1]

    def at_slot(k):
        return lambda i, tile_ids, slot_ids: (slot_ids[i * KT + k], 0, 0)

    return pl.pallas_call(
        attend_kernel,
        grid_spec=pltpu.PrefetchScalarGridSpec(
            num_scalar_prefetch=2,
            grid=(tiles,),
            in_specs=[pl.BlockSpec((TILE, width), lambda i, tile_ids, slot_ids: (tile_ids[i], 0))]
            + [pl.BlockSpec((1, TILE, 2 * width), at_slot(k)) for k in range(KT)],
            out_specs=pl.BlockSpec((TILE, width), lambda i, tile_ids, slot_ids: (i, 0)),
        ),
        out_shape=jax.ShapeDtypeStruct((tiles * TILE, width), jnp.bfloat16),
        compiler_params=pltpu.CompilerParams(vmem_limit_bytes=VMEM),
        cost_estimate=pl.CostEstimate(
            flops=4 * tiles * TILE * KT * TILE * width,
            bytes_accessed=2 * tiles * TILE * width * (2 + 2 * KT),
            transcendentals=tiles * TILE * KT * TILE * (width // HD),
        ),
    )(tile_ids, slot_ids, queries, *([buffer] * KT))


def request_lists(rows, shards, tile_count, capacity):
    entries = rows.reshape(-1)
    owned = (entries // tile_count)[None, :] == jnp.arange(shards, dtype=jnp.int32)[:, None]
    rank = jnp.cumsum(owned.astype(jnp.int32), axis=1) - 1
    slot_ids = jnp.arange(capacity, dtype=jnp.int32)
    select = owned[:, None, :] & (rank[:, None, :] == slot_ids[None, :, None])
    chosen = jnp.sum(jnp.where(select, (entries % tile_count)[None, None, :], 0), axis=2)
    return chosen, jnp.sum(jnp.where(owned, rank, 0), axis=0)


def pick_kernel(count, which, ids, *refs):
    sources, outs, sems = refs[:count], refs[count:-1], refs[-1]
    for at, source in enumerate(sources):

        @pl.when(which[0] == at)
        def _():
            copies = []
            for n, out in enumerate(outs):
                for j in range(out.shape[0]):
                    slot = n * out.shape[0] + j
                    copies.append(
                        pltpu.make_async_copy(source.at[ids[slot]], out.at[j], sems.at[slot])
                    )
            for copy in copies:
                copy.start()
            for copy in copies:
                copy.wait()


def pick(sources, which, lists):
    capacity = lists[0].shape[0]
    shape = jax.ShapeDtypeStruct((capacity,) + sources[0].shape[1:], sources[0].dtype)
    size = capacity * len(lists) * sources[0].shape[1] * sources[0].shape[2]
    return pl.pallas_call(
        lambda *refs: pick_kernel(len(sources), *refs),
        grid_spec=pltpu.PrefetchScalarGridSpec(
            num_scalar_prefetch=2,
            grid=(1,),
            in_specs=[pl.BlockSpec(memory_space=pl.ANY)] * len(sources),
            out_specs=[pl.BlockSpec(memory_space=pl.ANY)] * len(lists),
            scratch_shapes=[pltpu.SemaphoreType.DMA((capacity * len(lists),))],
        ),
        out_shape=[shape] * len(lists),
        cost_estimate=pl.CostEstimate(flops=0, bytes_accessed=4 * size, transcendentals=0),
    )(which.reshape(1), jnp.concatenate(lists), *sources)


def grid_body(tokens, norm_gain, in_weight, out_weight, pattern):
    shards = ZS * XS
    z, x = lax.axis_index("z"), lax.axis_index("x")
    y, c = lax.axis_index("y"), lax.axis_index("c")
    me, beside = z * XS + x, z * XS + (1 - x)
    rows, depth = tokens.shape
    tile_count = rows // TILE
    entries = tile_count * (KT - 1)
    capacity = max(2, 3 * entries // (2 * (shards - 1)))
    head_width = in_weight.shape[2]
    share = TILE // PARTS
    order = jnp.asarray(ORDER, jnp.int32)[z]
    step = capacity // 2

    def line(up, down, s):
        up = lax.ppermute(up, "z", [(i, i + 1) for i in range(s - 1, ZS - 1)])
        down = lax.ppermute(down, "z", [(i, i - 1) for i in range(1, ZS - s + 1)])
        return up, down

    def across(a):
        return lax.ppermute(a, "y", SWAP)

    def aside(a):
        return lax.ppermute(a, "c", SWAP)

    def over(a):
        return lax.ppermute(a, "x", SWAP)

    tiles = tokens.reshape(tile_count, PARTS, share, depth)
    mine = lax.dynamic_index_in_dim(tiles, y * CS + c, 1, keepdims=False)
    block = normalize(mine, norm_gain)
    ups, downs = {}, {}
    ups[1], downs[1] = line(block, block, 1)

    my_rows = lax.dynamic_slice_in_dim(pattern, me * tile_count, tile_count, 0)[:, 1:]
    beside_rows = lax.dynamic_slice_in_dim(pattern, beside * tile_count, tile_count, 0)[:, 1:]
    my_lists, my_rank = request_lists(my_rows, shards, tile_count, capacity)
    beside_lists, _ = request_lists(beside_rows, shards, tile_count, capacity)

    first = beside_lists[me] * PARTS + c
    both = jnp.concatenate([first + y * CS, first + (1 - y) * CS])
    rx0 = over(normalize(tokens.reshape(tile_count * PARTS, share, depth)[both], norm_gain))
    w_across = across(out_weight)

    normed = normalize(tokens, norm_gain)
    queries = jnp.dot(
        normed, in_weight[:, 0, :], preferred_element_type=jnp.float32
    ).astype(jnp.bfloat16)
    weight = in_weight[:, 1:, :].reshape(depth, 2 * head_width)
    slots = OWN_SLOTS + capacity * (2 * ZS - 1)
    buffer = project(
        [(normed.reshape(tile_count, TILE, depth), 0)], tile_count, weight, slots, 0, 4, None
    )

    def after(lists, *results):
        return lax.optimization_barrier((lists, results))[0]

    def choose(k, lists, sources, which):
        source = order[k] * XS + x
        return pick(sources, which, [rows[source] for rows in lists])

    def place(at, parts, buffer):
        base = OWN_SLOTS + at * capacity
        return project(parts, capacity, weight, slots, base, step, buffer)

    def quarters(a, b):
        return [(a, 0), (b, 0), (aside(a), 0), (aside(b), 0)]

    lists = after((my_lists, beside_lists), ups[1], downs[1], buffer, queries, w_across)
    ups[2], downs[2] = line(ups[1], downs[1], 2)
    own1, out1 = choose(1, lists, [downs[1], ups[1]], z % 2)
    rx1, own1y = over(out1), across(own1)
    side0 = aside(rx0)
    buffer = place(
        0, [(rx0, 0), (rx0, capacity), (side0, 0), (side0, capacity)], buffer
    )

    lists = after(lists, ups[2], downs[2], rx1, own1y, buffer)
    ups[3], downs[3] = line(ups[2], downs[2], 3)
    own2, out2 = choose(2, lists, [downs[2], downs[1], ups[1], ups[2]], z)
    rx1y, rx2, own2y = across(rx1), over(out2), across(own2)
    buffer = place(1, quarters(own1, own1y), buffer)
    buffer = place(2, quarters(rx1, rx1y), buffer)

    lists = after(lists, ups[3], downs[3], rx2, own2y, buffer)
    own3, out3 = choose(3, lists, [downs[3], downs[2], ups[2], ups[3]], z)
    rx2y, rx3, own3y = across(rx2), over(out3), across(own3)
    buffer = place(3, quarters(own2, own2y), buffer)
    buffer = place(4, quarters(rx2, rx2y), buffer)
    rx3y = across(rx3)
    buffer = place(5, quarters(own3, own3y), buffer)
    buffer = place(6, quarters(rx3, rx3y), buffer)
    out_all = jnp.concatenate(
        [out_weight, w_across, aside(out_weight), aside(w_across)], axis=0
    )

    owner = my_rows // tile_count
    step_of = jnp.sum(
        jnp.where(
            order[None, None, :] == (owner // XS)[:, :, None],
            jnp.arange(ZS, dtype=jnp.int32)[None, None, :],
            0,
        ),
        axis=2,
    )
    group = 2 * step_of - jnp.where(owner % XS == x, 1, 0)
    far_slots = OWN_SLOTS + group * capacity + my_rank.reshape(tile_count, KT - 1)
    slot_ids = jnp.concatenate(
        [jnp.arange(tile_count, dtype=jnp.int32)[:, None], far_slots], axis=1
    )

    half = tile_count // YS
    near = jnp.arange(half, dtype=jnp.int32)

    def attend_half(which):
        ids = which * half + near
        picked = lax.dynamic_slice_in_dim(slot_ids, which * half, half, 0)
        return attend(ids, picked.reshape(-1), queries, buffer)

    far_came = across(attend_half(1 - y))
    own = attend_half(y)
    quarter = own.shape[0] // CS
    keep = [lax.dynamic_slice_in_dim(a, c * quarter, quarter, 0) for a in (own, far_came)]
    give = [lax.dynamic_slice_in_dim(a, (1 - c) * quarter, quarter, 0) for a in (own, far_came)]
    attended = jnp.concatenate(keep + [aside(a) for a in give], axis=1)
    return jnp.dot(attended, out_all, preferred_element_type=jnp.float32).astype(jnp.bfloat16)


def solution(mesh):
    if mesh.devices.shape == (ZS * XS, YS * CS):
        grid = Mesh(mesh.devices.reshape(ZS, XS, YS, CS), ("z", "x", "y", "c"))
        seq, head = ("z", "x"), ("y", "c")
        return jax.shard_map(
            grid_body,
            mesh=grid,
            in_specs=(P(seq, None), P(), P(None, None, head), P(head, None), P()),
            out_specs=P(seq + head, None),
            check_vma=False,
        )
    return jax.shard_map(
        body,
        mesh=mesh,
        in_specs=(P("seq", None), P(), P(None, None, "head"), P("head", None), P()),
        out_specs=P(("seq", "head"), None),
        check_vma=False,
    )
```

```python
import math

import jax
import jax.numpy as jnp
from jax import lax
from jax.experimental import pallas as pl
from jax.experimental.pallas import tpu as pltpu
from jax.sharding import Mesh
from jax.sharding import PartitionSpec as P

HD = 128
TILE = 128
KT = 4
ZS, XS, YS, CS = 4, 2, 2, 2
PARTS = YS * CS
ORDER = ((0, 1, 2, 3), (1, 0, 2, 3), (2, 3, 1, 0), (3, 2, 1, 0))
SWAP = ((0, 1), (1, 0))
OWN_SLOTS = 20
VMEM = 48 * 1024 * 1024


def normalize(tokens, norm_gain):
    values = tokens.astype(jnp.float32)
    mean_square = jnp.mean(values * values, axis=-1, keepdims=True)
    return (values * lax.rsqrt(mean_square + 1e-05) * norm_gain).astype(jnp.bfloat16)


def by_request(keyvals, pattern, my_rows, shards, myself, tile_count):
    entries = tile_count * (KT - 1)
    capacity = max(2, 3 * entries // (2 * (shards - 1)))
    wanted = pattern.reshape(shards, tile_count, KT)[:, :, 1:].reshape(shards, entries)
    owners = wanted // tile_count
    local_tile = wanted % tile_count
    owned_here = owners == myself
    ranking = jnp.cumsum(owned_here.astype(jnp.int32), axis=1) - 1
    slot_ids = jnp.arange(capacity, dtype=jnp.int32)
    select = owned_here[:, None, :] & (ranking[:, None, :] == slot_ids[None, :, None])
    filled = jnp.any(select, axis=2)
    chosen = jnp.sum(jnp.where(select, local_tile[:, None, :], 0), axis=2)
    outgoing = jnp.where(filled[:, :, None, None], keyvals[chosen], jnp.zeros((), keyvals.dtype))
    incoming = lax.all_to_all(outgoing, "seq", split_axis=0, concat_axis=0, tiled=True)
    sources = my_rows[:, 1:].reshape(entries) // tile_count
    one_hot = (sources[:, None] == jnp.arange(shards, dtype=jnp.int32)[None, :]).astype(jnp.int32)
    running = jnp.cumsum(one_hot, axis=0)
    position = jnp.sum(running * one_hot, axis=1) - 1
    flat_index = sources * capacity + position
    fetched = incoming.reshape(shards * capacity, TILE, keyvals.shape[2])[flat_index]
    return fetched.reshape(tile_count, KT - 1, TILE, keyvals.shape[2])


def body(tokens, norm_gain, in_weight, out_weight, pattern):
    shards = lax.axis_size("seq")
    myself = lax.axis_index("seq")
    row_count = tokens.shape[0]
    tile_count = row_count // TILE
    head_width = in_weight.shape[2]
    head_count = head_width // HD
    normed = normalize(tokens, norm_gain)
    projected = jnp.dot(
        normed,
        in_weight.reshape(in_weight.shape[0], 3 * head_width),
        preferred_element_type=jnp.float32,
    ).astype(jnp.bfloat16)
    projected = projected.reshape(row_count, 3, head_width)
    queries = projected[:, 0].reshape(tile_count, TILE, head_count, HD)
    keyvals = jnp.concatenate([projected[:, 1], projected[:, 2]], axis=1).reshape(
        tile_count, TILE, 2 * head_width
    )
    my_rows = lax.dynamic_slice_in_dim(pattern, myself * tile_count, tile_count, 0)
    fetched = by_request(keyvals, pattern, my_rows, shards, myself, tile_count)
    gathered = jnp.concatenate([keyvals[:, None], fetched], axis=1).reshape(
        tile_count, KT * TILE, 2 * head_width
    )
    key_block = gathered[:, :, :head_width].reshape(tile_count, KT * TILE, head_count, HD)
    value_block = gathered[:, :, head_width:].reshape(tile_count, KT * TILE, head_count, HD)
    scores = jnp.einsum(
        "tqhd,tkhd->thqk", queries, key_block, preferred_element_type=jnp.float32
    ) * (1.0 / math.sqrt(HD))
    maxima = jnp.max(scores, axis=-1, keepdims=True)
    exponent = jnp.exp(scores - maxima)
    weights = (exponent / jnp.sum(exponent, axis=-1, keepdims=True)).astype(jnp.bfloat16)
    attended = jnp.einsum(
        "thqk,tkhd->tqhd", weights, value_block, preferred_element_type=jnp.float32
    ).astype(jnp.bfloat16)
    attended = attended.reshape(row_count, head_width)
    return lax.psum_scatter(
        jnp.dot(attended, out_weight, preferred_element_type=jnp.float32).astype(jnp.bfloat16),
        "head",
        scatter_dimension=0,
        tiled=True,
    )


def project_kernel(count, *refs):
    blocks, weight, out = refs[:count], refs[count], refs[-1]
    rows = jnp.concatenate([ref[...] for ref in blocks], axis=1)
    tiles, height, depth = rows.shape
    product = jnp.dot(
        rows.reshape(tiles * height, depth), weight[...], preferred_element_type=jnp.float32
    )
    out[...] = product.astype(out.dtype).reshape(tiles, height, out.shape[2])


def project(pieces, tiles, weight, slots, base, step, buffer):
    depth, width = weight.shape

    def rows_from(array, start):
        return pl.BlockSpec((step, array.shape[1], depth), lambda i: (start // step + i, 0, 0))

    in_specs = [rows_from(*piece) for piece in pieces]
    in_specs.append(pl.BlockSpec((depth, width), lambda i: (0, 0)))
    operands = [array for array, _ in pieces] + [weight]
    aliases = {}
    if buffer is not None:
        aliases = {len(operands): 0}
        in_specs.append(pl.BlockSpec(memory_space=pl.ANY))
        operands.append(buffer)
    rows = tiles * TILE
    return pl.pallas_call(
        lambda *refs: project_kernel(len(pieces), *refs),
        grid=(tiles // step,),
        in_specs=in_specs,
        out_specs=pl.BlockSpec((step, TILE, width), lambda i: (base // step + i, 0, 0)),
        out_shape=jax.ShapeDtypeStruct((slots, TILE, width), jnp.bfloat16),
        input_output_aliases=aliases,
        compiler_params=pltpu.CompilerParams(vmem_limit_bytes=VMEM),
        cost_estimate=pl.CostEstimate(
            flops=2 * rows * depth * width,
            bytes_accessed=2 * (rows * depth + depth * width + rows * width),
            transcendentals=0,
        ),
    )(*operands)


def project_own_kernel(block, weight, query_weight, mark, out, queries):
    project_kernel(1, block, weight, out)
    tiles, height, depth = block.shape
    queries[...] = jnp.dot(
        block[...].reshape(tiles * height, depth),
        query_weight[...],
        preferred_element_type=jnp.float32,
    ).astype(queries.dtype)


def project_own(normed, weight, query_weight, slots, step, mark):
    tiles, height, depth = normed.shape
    width, query_width = weight.shape[1], query_weight.shape[1]
    rows = tiles * height
    return pl.pallas_call(
        project_own_kernel,
        grid=(tiles // step,),
        in_specs=[
            pl.BlockSpec((step, height, depth), lambda i: (i, 0, 0)),
            pl.BlockSpec((depth, width), lambda i: (0, 0)),
            pl.BlockSpec((depth, query_width), lambda i: (0, 0)),
            pl.BlockSpec(memory_space=pl.ANY),
        ],
        out_specs=[
            pl.BlockSpec((step, height, width), lambda i: (i, 0, 0)),
            pl.BlockSpec((step * height, query_width), lambda i: (i, 0)),
        ],
        out_shape=[
            jax.ShapeDtypeStruct((slots, height, width), jnp.bfloat16),
            jax.ShapeDtypeStruct((rows, query_width), jnp.bfloat16),
        ],
        compiler_params=pltpu.CompilerParams(vmem_limit_bytes=VMEM),
        cost_estimate=pl.CostEstimate(
            flops=2 * rows * depth * (width + query_width),
            bytes_accessed=2 * (rows + depth) * (depth + width + query_width),
            transcendentals=0,
        ),
    )(normed, weight, query_weight, mark)


def attend_kernel(tile_ids, slot_ids, query, *refs):
    blocks, out = refs[:KT], refs[KT]
    width = query.shape[1]
    for head in range(width // HD):
        at = slice(head * HD, (head + 1) * HD)
        at_value = slice(width + head * HD, width + (head + 1) * HD)
        keys = jnp.concatenate([ref[0, :, at] for ref in blocks], axis=0)
        values = jnp.concatenate([ref[0, :, at_value] for ref in blocks], axis=0)
        scores = lax.dot_general(
            query[:, at], keys, (((1,), (1,)), ((), ())), preferred_element_type=jnp.float32
        )
        maxima = jnp.max(scores, axis=-1, keepdims=True)
        exponent = jnp.exp2((scores - maxima) * (math.log2(math.e) / math.sqrt(HD)))
        total = jnp.sum(exponent, axis=-1, keepdims=True)
        summed = jnp.dot(
            exponent.astype(jnp.bfloat16), values, preferred_element_type=jnp.float32
        )
        out[:, at] = (summed / total).astype(out.dtype)


def attend(tile_ids, slot_ids, queries, buffer):
    tiles, width = tile_ids.shape[0], queries.shape[1]

    def at_slot(k):
        return lambda i, tile_ids, slot_ids: (slot_ids[i * KT + k], 0, 0)

    return pl.pallas_call(
        attend_kernel,
        grid_spec=pltpu.PrefetchScalarGridSpec(
            num_scalar_prefetch=2,
            grid=(tiles,),
            in_specs=[pl.BlockSpec((TILE, width), lambda i, tile_ids, slot_ids: (tile_ids[i], 0))]
            + [pl.BlockSpec((1, TILE, 2 * width), at_slot(k)) for k in range(KT)],
            out_specs=pl.BlockSpec((TILE, width), lambda i, tile_ids, slot_ids: (i, 0)),
        ),
        out_shape=jax.ShapeDtypeStruct((tiles * TILE, width), jnp.bfloat16),
        compiler_params=pltpu.CompilerParams(vmem_limit_bytes=VMEM),
        cost_estimate=pl.CostEstimate(
            flops=4 * tiles * TILE * KT * TILE * width,
            bytes_accessed=2 * tiles * TILE * width * (2 + 2 * KT),
            transcendentals=tiles * TILE * KT * TILE * (width // HD),
        ),
    )(tile_ids, slot_ids, queries, *([buffer] * KT))


def request_lists(rows, shards, tile_count, capacity):
    entries = rows.reshape(-1)
    owned = (entries // tile_count)[None, :] == jnp.arange(shards, dtype=jnp.int32)[:, None]
    rank = jnp.cumsum(owned.astype(jnp.int32), axis=1) - 1
    slot_ids = jnp.arange(capacity, dtype=jnp.int32)
    select = owned[:, None, :] & (rank[:, None, :] == slot_ids[None, :, None])
    chosen = jnp.sum(jnp.where(select, (entries % tile_count)[None, None, :], 0), axis=2)
    return chosen, jnp.sum(jnp.where(owned, rank, 0), axis=0)


def pick_kernel(count, which, ids, *refs):
    sources, outs, sems = refs[:count], refs[count:-1], refs[-1]
    for at, source in enumerate(sources):

        @pl.when(which[0] == at)
        def _():
            copies = []
            for n, out in enumerate(outs):
                for j in range(out.shape[0]):
                    slot = n * out.shape[0] + j
                    copies.append(
                        pltpu.make_async_copy(source.at[ids[slot]], out.at[j], sems.at[slot])
                    )
            for copy in copies:
                copy.start()
            for copy in copies:
                copy.wait()


def pick(sources, which, lists):
    capacity = lists[0].shape[0]
    shape = jax.ShapeDtypeStruct((capacity,) + sources[0].shape[1:], sources[0].dtype)
    size = capacity * len(lists) * sources[0].shape[1] * sources[0].shape[2]
    return pl.pallas_call(
        lambda *refs: pick_kernel(len(sources), *refs),
        grid_spec=pltpu.PrefetchScalarGridSpec(
            num_scalar_prefetch=2,
            grid=(1,),
            in_specs=[pl.BlockSpec(memory_space=pl.ANY)] * len(sources),
            out_specs=[pl.BlockSpec(shape.shape, lambda i, which, ids: (0, 0, 0))] * len(lists),
            scratch_shapes=[pltpu.SemaphoreType.DMA((capacity * len(lists),))],
        ),
        out_shape=[shape] * len(lists),
        compiler_params=pltpu.CompilerParams(vmem_limit_bytes=VMEM),
        cost_estimate=pl.CostEstimate(flops=0, bytes_accessed=4 * size, transcendentals=0),
    )(which.reshape(1), jnp.concatenate(lists), *sources)


def grid_body(tokens, norm_gain, in_weight, out_weight, pattern):
    shards = ZS * XS
    z, x = lax.axis_index("z"), lax.axis_index("x")
    y, c = lax.axis_index("y"), lax.axis_index("c")
    me, beside = z * XS + x, z * XS + (1 - x)
    rows, depth = tokens.shape
    tile_count = rows // TILE
    entries = tile_count * (KT - 1)
    capacity = max(2, 3 * entries // (2 * (shards - 1)))
    head_width = in_weight.shape[2]
    share = TILE // PARTS
    order = jnp.asarray(ORDER, jnp.int32)[z]
    step = capacity // 2

    def line(up, down, s):
        up = lax.ppermute(up, "z", [(i, i + 1) for i in range(s - 1, ZS - 1)])
        down = lax.ppermute(down, "z", [(i, i - 1) for i in range(1, ZS - s + 1)])
        return up, down

    def across(a, *results):
        if results:
            a = lax.optimization_barrier((a, results))[0]
        return lax.ppermute(a, "y", SWAP)

    def aside(a):
        return lax.ppermute(a, "c", SWAP)

    def over(a):
        return lax.ppermute(a, "x", SWAP)

    tiles = tokens.reshape(tile_count, PARTS, share, depth)
    mine = lax.dynamic_index_in_dim(tiles, y * CS + c, 1, keepdims=False)
    block = normalize(mine, norm_gain)
    ups, downs = {}, {}
    ups[1], downs[1] = line(block, block, 1)

    my_rows = lax.dynamic_slice_in_dim(pattern, me * tile_count, tile_count, 0)[:, 1:]
    beside_rows = lax.dynamic_slice_in_dim(pattern, beside * tile_count, tile_count, 0)[:, 1:]
    my_lists, my_rank = request_lists(my_rows, shards, tile_count, capacity)
    beside_lists, _ = request_lists(beside_rows, shards, tile_count, capacity)

    first = beside_lists[me] * PARTS + c
    both = jnp.concatenate([first + y * CS, first + (1 - y) * CS])
    rx0 = over(normalize(tokens.reshape(tile_count * PARTS, share, depth)[both], norm_gain))
    w_across = across(out_weight)

    normed = normalize(tokens, norm_gain)
    query_weight = in_weight[:, 0, :]
    weight = in_weight[:, 1:, :].reshape(depth, 2 * head_width)
    slots = OWN_SLOTS + capacity * (2 * ZS - 1)

    def after(lists, *results):
        return lax.optimization_barrier((lists, results))[0]

    def choose(k, lists, sources, which):
        source = order[k] * XS + x
        return pick(sources, which, [rows[source] for rows in lists])

    def place(at, parts, buffer):
        base = OWN_SLOTS + at * capacity
        return project(parts, capacity, weight, slots, base, step, buffer)

    def quarters(a, b):
        return [(a, 0), (b, 0), (aside(a), 0), (aside(b), 0)]

    lists = after((my_lists, beside_lists), ups[1], downs[1], normed, weight, w_across)
    ups[2], downs[2] = line(ups[1], downs[1], 2)
    own1, out1 = choose(1, lists, [downs[1], ups[1]], z % 2)
    rx1, own1y = over(out1), across(own1, rx0, w_across)
    side0 = aside(rx0)
    buffer, queries = project_own(
        normed.reshape(tile_count, TILE, depth), weight, query_weight, slots, 4, lists[0]
    )
    buffer = place(
        0, [(rx0, 0), (rx0, capacity), (side0, 0), (side0, capacity)], buffer
    )

    lists = after(lists, ups[2], downs[2], rx1, own1y, buffer)
    ups[3], downs[3] = line(ups[2], downs[2], 3)
    own2, out2 = choose(2, lists, [downs[2], downs[1], ups[1], ups[2]], z)
    rx2, rx1y = over(out2), across(rx1, own1y)
    own2y = across(own2, rx1y)
    buffer = place(1, quarters(own1, own1y), buffer)
    buffer = place(2, quarters(rx1, rx1y), buffer)

    lists = after(lists, ups[3], downs[3], rx2)
    own3, out3 = choose(3, lists, [downs[3], downs[2], ups[2], ups[3]], z)
    rx3, rx2y = over(out3), across(rx2, own2y)
    own3y = across(own3, rx2y)
    buffer = place(3, quarters(own2, own2y), buffer)
    rx3y = across(rx3, own3y, buffer)
    buffer = place(4, quarters(rx2, rx2y), buffer)
    buffer = place(5, quarters(own3, own3y), buffer)
    rx3y, _ = lax.optimization_barrier((rx3y, buffer))
    buffer = place(6, quarters(rx3, rx3y), buffer)
    out_all = jnp.concatenate(
        [out_weight, w_across, aside(out_weight), aside(w_across)], axis=0
    )

    owner = my_rows // tile_count
    step_of = jnp.sum(
        jnp.where(
            order[None, None, :] == (owner // XS)[:, :, None],
            jnp.arange(ZS, dtype=jnp.int32)[None, None, :],
            0,
        ),
        axis=2,
    )
    group = 2 * step_of - jnp.where(owner % XS == x, 1, 0)
    far_slots = OWN_SLOTS + group * capacity + my_rank.reshape(tile_count, KT - 1)
    slot_ids = jnp.concatenate(
        [jnp.arange(tile_count, dtype=jnp.int32)[:, None], far_slots], axis=1
    )

    half = tile_count // YS
    near = jnp.arange(half, dtype=jnp.int32)

    def attend_half(which):
        ids = which * half + near
        picked = lax.dynamic_slice_in_dim(slot_ids, which * half, half, 0)
        return attend(ids, picked.reshape(-1), queries, buffer)

    far_came = across(attend_half(1 - y))
    own = attend_half(y)
    quarter = own.shape[0] // CS
    keep = [lax.dynamic_slice_in_dim(a, c * quarter, quarter, 0) for a in (own, far_came)]
    give = [lax.dynamic_slice_in_dim(a, (1 - c) * quarter, quarter, 0) for a in (own, far_came)]
    attended = jnp.concatenate(keep + [aside(a) for a in give], axis=1)
    return jnp.dot(attended, out_all, preferred_element_type=jnp.float32).astype(jnp.bfloat16)


def solution(mesh):
    if mesh.devices.shape == (ZS * XS, YS * CS):
        grid = Mesh(mesh.devices.reshape(ZS, XS, YS, CS), ("z", "x", "y", "c"))
        seq, head = ("z", "x"), ("y", "c")
        return jax.shard_map(
            grid_body,
            mesh=grid,
            in_specs=(P(seq, None), P(), P(None, None, head), P(head, None), P()),
            out_specs=P(seq + head, None),
            check_vma=False,
        )
    return jax.shard_map(
        body,
        mesh=mesh,
        in_specs=(P("seq", None), P(), P(None, None, "head"), P("head", None), P()),
        out_specs=P(("seq", "head"), None),
        check_vma=False,
    )
```
